512 devices in a mesh: facet: 16 (over x_lo, y, core), pulse: 32 (over x_hi, z).
Axes of the slice: x: 4 (x_hi: 2, x_lo: 2; x = x_hi * 2 + x_lo), y: 4, z: 16, core: 2. Of those that a mesh axis runs over, the one named last changes fastest.
Arguments:
- facet_positions: float32 [3, 12288], P(None, 'facet'), may hold values from -10 to 10
- reflectivity: float32 [2, 12288], P(None, 'facet'), may hold values from -0.078125 to 0.078125
- block_building: int32 [96], P('facet'), may hold values from 0 to 23, never falling along the last dimension, each value on 1 to 8 neighbouring positions
- visible: int32 [24, 64], P(None, 'pulse'), may hold values from 0 to 1
- platform: float32 [3, 2048], P(None, 'pulse'), may hold values from 30 to 40
Outputs:
- image: float32 [2, 512, 2048], P(None, 'pulse', 'facet')
The draws below stay inside these ranges and needn't reach their ends.
All inputs are finite; a program needn't handle non-finite values.
Results may differ from the reference program's by a relative error of at most 0.017.
Values may be sent and summed in bfloat16 or wider, within the bound.
A program may use at most 64 MiB of HBM per device.

```python
import math
import jax
import jax.numpy as jnp
import numpy as np
from jax import lax

BLK = 128
PULSES = 2048
PBS = 32
BINS = 512
BIN_LO = 32
BMOST = 8
BIN_HI = 16
FACETS = 12288
FBLK = 96
NBLD = 24
PBLOCKS = 64


def draw_visible(key, part):
    key_first, key_length = jax.random.split(jax.random.fold_in(key, 7))
    first_block = jax.random.randint(key_first, (NBLD, 1), 0, PBLOCKS)
    run_length = jax.random.randint(key_length, (NBLD, 1), max(PBLOCKS // 8, 1), PBLOCKS + 1)
    blocks = jnp.arange(PBLOCKS, dtype=jnp.int32)[None, :]
    return ((blocks - first_block) % PBLOCKS < run_length).astype(jnp.int32)


def levels(own_key, shape, shards, least, top_value):
    loudness, own = 1.0, jax.random.fold_in(own_key, 6)
    for axis_at, blocks in shards:
        steps = jnp.exp(jax.random.uniform(jax.random.fold_in(own, axis_at), (blocks,), jnp.float32, least / len(shards), top_value / len(shards)))
        loudness = loudness * jnp.repeat(steps, shape[axis_at] // blocks).reshape([-1 if axis == axis_at else 1 for axis in range(len(shape))])
    return loudness


def split_up(number_of, total, bound, skew):
    weights = [(1 << 20) // math.isqrt(standing ** skew) + 1 for standing in range(2, number_of + 1)]
    spare, given = total - bound - (number_of - 1), [1] * (number_of - 1)
    while spare > 0:
        movable = [i for i in range(number_of - 1) if given[i] < bound]
        whole, left = sum([weights[i] for i in movable]), spare
        for i in movable:
            addition = min(bound - given[i], max(1, left * weights[i] // whole), spare)
            given[i] = given[i] + addition
            spare = spare - addition
    return np.array([bound] + given)


def uneven_parts(stream_key, number_of, total, most, skew):
    if number_of == 2:
        one = jax.random.randint(stream_key, (), max(1, total - most), min(most, total - 1) + 1)
        return jnp.stack([one, total - one])
    tallies = jnp.asarray(split_up(number_of, total, most, skew), jnp.int32)
    twos = (number_of - 1) // 2
    donor, sink = tallies[1:1 + 2 * twos:2], tallies[2:2 + 2 * twos:2]
    room = jnp.minimum(donor - 1, most - sink)
    passed = jax.random.randint(jax.random.fold_in(stream_key, 1), (twos,), 0, 1 << 20) % (room + 1)
    tallies = tallies.at[1:1 + 2 * twos:2].set(donor - passed).at[2:2 + 2 * twos:2].set(sink + passed)
    return tallies[jax.random.permutation(jax.random.fold_in(stream_key, 2), number_of)]


def bell_draw(stream_key, extent, width, limit, cuts=(), kind=jnp.bfloat16):
    drawn = jax.random.normal(stream_key, extent, jnp.float32) * width
    if len(cuts) > 0:
        drawn = levels(stream_key, extent, cuts, -0.22, 0.18) * drawn
    return jnp.clip(drawn, min=-limit, max=limit).astype(kind)


def setup_inputs(seed: int = 0) -> dict:
    keys = jax.random.split(jax.random.key(seed), 6)
    return {
        "facet_positions": jnp.clip(jax.random.uniform(keys[0], (3, FACETS), jnp.float32, -10.0, 10.0) * levels(keys[0], (3, FACETS), ((1, 16),), -0.4, 0.0), -10.0, 10.0),
        "reflectivity": bell_draw(keys[1], (2, FACETS), (FACETS // 2) ** -0.5, 0.078125, ((1, 16),), jnp.float32),
        "block_building": jnp.searchsorted(jnp.cumsum(uneven_parts(keys[2], NBLD, FBLK, BMOST, 2)), jnp.arange(FBLK), side="right").astype(jnp.int32),
        "visible": draw_visible(jax.random.fold_in(keys[5], 71), 0),
        "platform": jnp.clip(30.0 + 10.0 * jax.random.uniform(keys[4], (3, PULSES), jnp.float32) ** levels(keys[4], (3, PULSES), ((1, 32),), -0.2, 0.2), 30.0, 40.0),
    }


wave_start = 2.0
wave_step = 0.25

def echo_group(positions, weights, antenna):
    offsets = positions[:, None, :] - antenna[:, :, None]
    distance = jnp.sqrt(lax.optimization_barrier(jnp.sum(offsets * offsets, axis=0)))
    upper_index = jnp.arange(BIN_HI, dtype=jnp.float32)
    lower_index = jnp.arange(BIN_LO, dtype=jnp.float32)
    coarse = (wave_start + wave_step * BIN_LO * upper_index)[None, :, None] * distance[:, None, :]
    cosine = jnp.cos(coarse)
    sine_a = jnp.sin(coarse)
    real_a = weights[0][None, None, :] * cosine + weights[1][None, None, :] * sine_a
    imag_a = weights[1][None, None, :] * cosine - weights[0][None, None, :] * sine_a
    table_a = jnp.concatenate([real_a, imag_a], axis=1).astype(jnp.bfloat16)
    phase_b = (wave_step * lower_index)[None, :, None] * distance[:, None, :]
    table_b = jnp.concatenate([jnp.cos(phase_b), -jnp.sin(phase_b)], axis=1).astype(jnp.bfloat16)
    products = jnp.einsum('gan,gbn->gab', table_a.astype(jnp.float32), table_b.astype(jnp.float32))
    real_part = products[:, :BIN_HI, :BIN_LO] - products[:, BIN_HI:, BIN_LO:]
    imag_part = products[:, :BIN_HI, BIN_LO:] + products[:, BIN_HI:, :BIN_LO]
    return jnp.stack([real_part, imag_part]).reshape(2, antenna.shape[1], BINS)

def chirp_apply(spectrum, bin_rows, k_rows):
    offset_k = (k_rows - PULSES // 2).astype(jnp.float32)
    wave_bin = wave_start + wave_step * bin_rows.astype(jnp.float32)
    phase = jnp.pi * (offset_k * offset_k / PULSES)[None, :] * (wave_start / wave_bin)[:, None]
    cosine = jnp.cos(phase)
    sine_h = jnp.sin(phase)
    return jnp.stack([cosine * spectrum[0] - sine_h * spectrum[1], cosine * spectrum[1] + sine_h * spectrum[0]])

def reference(facet_positions, reflectivity, block_building, visible, platform):
    group_len = 8
    building_of = jnp.repeat(block_building, BLK)

    def one_group(group_index):
        first_pulse = group_index * group_len
        antenna = lax.dynamic_slice_in_dim(platform, first_pulse, group_len, 1)
        column = lax.dynamic_index_in_dim(visible, first_pulse // PBS, 1, keepdims=False)
        seen = jnp.take(column, building_of, axis=0).astype(jnp.float32)
        weights = reflectivity * seen[None, :]
        return echo_group(facet_positions, weights, antenna)
    groups = lax.map(one_group, jnp.arange(PULSES // group_len, dtype=jnp.int32))
    echo = groups.transpose(1, 3, 0, 2).reshape(2, BINS, PULSES)
    echo_b = echo.astype(jnp.bfloat16)
    k_rows = jnp.arange(PULSES, dtype=jnp.int32)
    angle_grid = 2.0 * math.pi / PULSES * (k_rows[:, None] * k_rows[None, :] % PULSES).astype(jnp.float32)
    scale_w = 1.0 / math.sqrt(PULSES)
    w_real = (jnp.cos(angle_grid) * scale_w).astype(jnp.bfloat16)
    w_imag = (-jnp.sin(angle_grid) * scale_w).astype(jnp.bfloat16)
    real_s = jnp.dot(echo_b[0], w_real.T, preferred_element_type=jnp.float32) - jnp.dot(echo_b[1], w_imag.T, preferred_element_type=jnp.float32)
    imag_s = jnp.dot(echo_b[0], w_imag.T, preferred_element_type=jnp.float32) + jnp.dot(echo_b[1], w_real.T, preferred_element_type=jnp.float32)
    spectrum = jnp.stack([real_s, imag_s])
    return chirp_apply(spectrum, jnp.arange(BINS, dtype=jnp.int32), k_rows)
```

```python
import functools
import math

import jax
import jax.numpy as jnp
from jax import lax
from jax.experimental import pallas as pl
from jax.experimental.pallas import tpu as pltpu
from jax.sharding import PartitionSpec as P

PULSES = 2048
F32 = jnp.float32
BF16 = jnp.bfloat16
TILES = 6
TURN = 1.0 / (2.0 * math.pi)

SIN_POLY = (3.1415926401307086, -5.167710083507905, 2.5500775232148403, -0.5982912856219295, 0.07765766030867731)
COS_POLY = (0.9999999532476086, -4.934792830619651, 4.058411352862725, -1.3318765680816778, 0.21968961109948743)


def horner(q, coefs):
    out = jnp.full_like(q, coefs[-1])
    for c in coefs[-2::-1]:
        out = out * q + c
    return out


def cos_sin_turns(u):
    r = u - jnp.round(u)
    q = r * r
    s = horner(q, SIN_POLY) * r
    c = horner(q, COS_POLY)
    t = s + s
    return 1.0 - t * s, t * c


def iota(shape, dim):
    return lax.broadcasted_iota(jnp.int32, shape, dim)


def kernel(
    fp_hbm, rf_hbm, bb_hbm, vis_hbm, plat_hbm, out_ref,
    fp, rf, bb, vis, plat, pcols, wts, ta, tb, send1, recv1, send2, recv2, recv3, wtab, chirp,
    in_sem, send_sem, recv_sem,
):
    j = lax.axis_index("facet")
    i = lax.axis_index("pulse")
    xl, y, core = j // 8, (j // 2) % 4, j % 2
    xh, z = i // 16, i % 16
    chip_facet = (j // 2) * 2

    ins = [
        pltpu.make_async_copy(src, dst, in_sem.at[n])
        for n, (src, dst) in enumerate(
            ((plat_hbm, plat), (fp_hbm, fp), (bb_hbm, bb), (vis_hbm, vis), (rf_hbm, rf))
        )
    ]
    for c in ins:
        c.start()

    barrier = pltpu.get_barrier_semaphore()
    for t in range(1, 16):
        pl.semaphore_signal(
            barrier, inc=1, device_id={"facet": (j + t) % 16, "pulse": i},
            device_id_type=pl.DeviceIdType.MESH,
        )
    for zs in range(16):
        pl.semaphore_signal(
            barrier, inc=1, device_id={"facet": chip_facet + xh, "pulse": 16 * (1 - core) + zs},
            device_id_type=pl.DeviceIdType.MESH,
        )

    for c in ins:
        c.wait()
    eye = iota((64, 64), 0) == iota((64, 64), 1)
    for d in range(3):
        column = jnp.sum(jnp.where(eye, plat[d : d + 1, :], 0.0), axis=1, keepdims=True)
        pcols[d] = jnp.broadcast_to(column, (64, 128))
    for blk in range(TILES):
        b = bb[blk]
        cols = pl.ds(blk * 128, 128)
        for h in range(2):
            seen = vis[b, h].astype(F32)
            wts[h, :, cols] = rf[:, cols] * seen

    lane = iota((128, 128), 1)
    same_pulse = (iota((128, 128), 0) % 8) == (lane % 8)
    fold = (iota((16, 128), 0) == iota((16, 128), 1) // 8).astype(BF16)
    scale_u = 0.125 * TURN
    for t in range(8):
        tx, ty = 1 - t // 4, (t % 4 + 1) % 4
        g = ((xl + tx) % 2) * 4 + (y + ty) % 4
        rows = pl.ds(pl.multiple_of(g * 8, 8), 8)
        px, py, pz = pcols[0, rows, :], pcols[1, rows, :], pcols[2, rows, :]
        half = g // 4
        buf = t % 2
        for n in range(TILES):
            cols = pl.ds(n * 128, 128)
            dx = fp[0:1, cols] - px
            dy = fp[1:2, cols] - py
            dz = fp[2:3, cols] - pz
            d2 = dx * dx + dy * dy + dz * dz
            u = jnp.sqrt(d2) * scale_u
            w0 = wts[half, 0:1, cols]
            w1 = wts[half, 1:2, cols]
            c0, s0 = cos_sin_turns(u)
            cz, sz = cos_sin_turns(64.0 * u)
            two = 4.0 * (c0 * c0) - 2.0
            cb, sb = [c0], [s0]
            cp, sp = c0, -s0
            for _ in range(15):
                cn, sn = two * cb[-1] - cp, two * sb[-1] - sp
                cp, sp = cb[-1], sb[-1]
                cb.append(cn)
                sb.append(sn)
            arp, aip = w0 * cb[8] - w1 * sb[8], w1 * cb[8] + w0 * sb[8]
            ar = [arp * cz + aip * sz]
            ai = [aip * cz - arp * sz]
            two_z = cz + cz
            for _ in range(15):
                rn, im = two_z * ar[-1] - arp, two_z * ai[-1] - aip
                arp, aip = ar[-1], ai[-1]
                ar.append(rn)
                ai.append(im)
            for m in range(0, 16, 2):
                r16 = slice(m * 8, m * 8 + 16)
                q16 = slice(128 + m * 8, 128 + m * 8 + 16)
                tb[buf, r16, cols] = jnp.concatenate([cb[m], cb[m + 1]], axis=0).astype(BF16)
                tb[buf, q16, cols] = jnp.concatenate([sb[m], sb[m + 1]], axis=0).astype(BF16)
                ta[buf, r16, cols] = jnp.concatenate([ar[m], ar[m + 1]], axis=0).astype(BF16)
                ta[buf, q16, cols] = jnp.concatenate([ai[m], ai[m + 1]], axis=0).astype(BF16)
        prod = lax.dot_general(
            ta[buf], tb[buf], (((1,), (1,)), ((), ())), preferred_element_type=F32
        )
        rc, rs = prod[:128, :128], prod[:128, 128:]
        ic, is_ = prod[128:, :128], prod[128:, 128:]
        parts = []
        for comp in (rc - is_, ic + rs, rc + is_, ic - rs):
            parts.append(jnp.where(same_pulse, comp, 0.0).astype(BF16))
        echo = lax.dot_general(
            fold, jnp.concatenate(parts, axis=1), (((1,), (0,)), ((), ())),
            preferred_element_type=F32,
        )
        for h in range(2):
            for pair in range(2):
                a = echo[8 * h : 8 * h + 8, pair * 256 : pair * 256 + 128]
                b = echo[8 * h : 8 * h + 8, pair * 256 + 128 : pair * 256 + 256]
                send1[t, h, pair * 16 : pair * 16 + 16, :] = jnp.concatenate([a, b], axis=0).astype(BF16)
        if t == 0:
            pl.semaphore_wait(barrier, 31)
        if t < 7:
            for h in range(2):
                pltpu.make_async_remote_copy(
                    src_ref=send1.at[t, h], dst_ref=recv1.at[2 * t + core],
                    send_sem=send_sem.at[0], recv_sem=recv_sem.at[0],
                    device_id={"facet": g * 2 + h, "pulse": i},
                    device_id_type=pl.DeviceIdType.MESH,
                ).start()
        else:
            pltpu.make_async_remote_copy(
                src_ref=send1.at[7, 1 - core], dst_ref=recv1.at[14],
                send_sem=send_sem.at[0], recv_sem=recv_sem.at[0],
                device_id={"facet": g * 2 + 1 - core, "pulse": i},
                device_id_type=pl.DeviceIdType.MESH,
            ).start()

    lanes = iota((1, 512), 1)
    owner = (j + 1 + lanes // 32) % 16
    first = 64 * (16 * (1 - owner % 2) + lanes % 16) + 8 * (owner // 2) + 4 * (lanes // 16 % 2)
    first = first.astype(F32)
    norm = 1.0 / math.sqrt(PULSES)

    def weight_rows(m, carry):
        k = (j * 128 + m * 16 + iota((16, 512), 0)).astype(F32)
        wr, wi = cos_sin_turns(k * first * (1.0 / PULSES))
        wr, wi = wr * norm, -wi * norm
        er, ei = cos_sin_turns(k * (1.0 / PULSES))
        rows = pl.ds(pl.multiple_of(m * 16, 16), 16)
        rows_i = pl.ds(pl.multiple_of(128 + m * 16, 16), 16)
        for q in range(4):
            wtab[q, rows, :] = wr.astype(BF16)
            wtab[q, rows_i, :] = wi.astype(BF16)
            wr, wi = wr * er + wi * ei, wi * er - wr * ei
        return carry

    lax.fori_loop(0, 8, weight_rows, 0)

    row = iota((256, 256), 0)
    col = iota((256, 256), 1)
    comp_r, bin_r, pulse_r = row // 128, row // 8 % 16, row % 8
    comp_c, bin_c, pulse_c = col // 16 % 2, col % 16, col // 32
    same = jnp.logical_and(comp_r == comp_c, pulse_r == pulse_c)
    turn_up = jnp.where(jnp.logical_and(same, bin_r == bin_c), 1.0, 0.0).astype(BF16)
    turn_down = jnp.where(jnp.logical_and(same, bin_r == 15 - bin_c), 1.0, 0.0).astype(BF16)

    got1 = pltpu.make_async_remote_copy(
        src_ref=recv1, dst_ref=recv1, send_sem=send_sem.at[0], recv_sem=recv_sem.at[0],
        device_id={"facet": j, "pulse": i}, device_id_type=pl.DeviceIdType.MESH,
    )
    got1.wait_recv()
    total = send1[7, core].astype(F32)
    for s in range(15):
        total = total + recv1[s].astype(F32)
    for sign, turn in ((0, turn_down), (1, turn_up)):
        lo = sign * 16
        pieces = jnp.concatenate([total[lo : lo + 8], total[lo + 8 : lo + 16]], axis=1).astype(BF16)
        turned = jnp.dot(pieces, turn, preferred_element_type=F32)
        for a in range(8):
            for ph in range(2):
                send2[2 * a + sign, ph : ph + 1, :] = turned[a : a + 1, ph * 128 : ph * 128 + 128]
    for t in range(16):
        zd = (z + t) % 16
        pltpu.make_async_remote_copy(
            src_ref=send2.at[zd], dst_ref=recv2.at[z],
            send_sem=send_sem.at[1], recv_sem=recv_sem.at[1],
            device_id={"facet": chip_facet + 1 - xh, "pulse": 16 * core + zd},
            device_id_type=pl.DeviceIdType.MESH,
        ).start()

    kk = (j * 128 - PULSES // 2 + iota((16, 128), 1)).astype(F32)
    ff = (i * 16 + iota((16, 128), 0)).astype(F32)
    ch_c, ch_s = cos_sin_turns(kk * kk * (1.0 / PULSES) / (2.0 + 0.25 * ff))
    chirp[0] = ch_c
    chirp[1] = ch_s

    got2 = pltpu.make_async_remote_copy(
        src_ref=send2, dst_ref=recv2, send_sem=send_sem.at[1], recv_sem=recv_sem.at[1],
        device_id={"facet": j, "pulse": i}, device_id_type=pl.DeviceIdType.MESH,
    )
    got2.wait_recv()
    recv3[15] = jnp.concatenate([recv2[:, 0, :], recv2[:, 1, :]], axis=0).astype(BF16)
    for t in range(1, 16):
        pltpu.make_async_remote_copy(
            src_ref=recv3.at[15], dst_ref=recv3.at[15 - t],
            send_sem=send_sem.at[2], recv_sem=recv_sem.at[2],
            device_id={"facet": (j + t) % 16, "pulse": i},
            device_id_type=pl.DeviceIdType.MESH,
        ).start()
    got3 = pltpu.make_async_remote_copy(
        src_ref=recv3.at[pl.ds(0, 15)], dst_ref=recv3.at[pl.ds(0, 15)],
        send_sem=send_sem.at[2], recv_sem=recv_sem.at[2],
        device_id={"facet": j, "pulse": i}, device_id_type=pl.DeviceIdType.MESH,
    )
    got3.wait_recv()

    held = recv3[...].reshape(512, 128)
    slot = iota((256, 128), 1) // 32
    acc = jnp.zeros((256, 128), F32)
    for q in range(4):
        full = jnp.dot(wtab[q], held, preferred_element_type=F32)
        acc = jnp.where(slot == q, full, acc)
    flat = acc.T
    summed = flat[0:32] + flat[32:64] + flat[64:96] + flat[96:128]
    re = summed[0:16, 0:128] - summed[16:32, 128:256]
    im = summed[0:16, 128:256] + summed[16:32, 0:128]
    out_ref[0] = chirp[0] * re - chirp[1] * im
    out_ref[1] = chirp[0] * im + chirp[1] * re

    got1.wait_send()
    got2.wait_send()
    got3.wait_send()


def body(facet_positions, reflectivity, block_building, visible, platform):
    anywhere = pl.BlockSpec(memory_space=pl.ANY)
    return pl.pallas_call(
        kernel,
        out_shape=jax.ShapeDtypeStruct((2, 16, 128), F32),
        in_specs=[anywhere] * 5,
        out_specs=pl.BlockSpec(memory_space=pltpu.VMEM),
        scratch_shapes=[
            pltpu.VMEM((3, 768), F32),
            pltpu.VMEM((2, 768), F32),
            pltpu.SMEM((6,), jnp.int32),
            pltpu.SMEM((24, 2), jnp.int32),
            pltpu.VMEM((3, 64), F32),
            pltpu.VMEM((3, 64, 128), F32),
            pltpu.VMEM((2, 2, 768), F32),
            pltpu.VMEM((2, 256, 768), BF16),
            pltpu.VMEM((2, 256, 768), BF16),
            pltpu.VMEM((8, 2, 32, 128), BF16),
            pltpu.VMEM((15, 32, 128), BF16),
            pltpu.VMEM((16, 2, 128), F32),
            pltpu.VMEM((16, 2, 128), F32),
            pltpu.VMEM((16, 32, 128), BF16),
            pltpu.VMEM((4, 256, 512), BF16),
            pltpu.VMEM((2, 16, 128), F32),
            pltpu.SemaphoreType.DMA((5,)),
            pltpu.SemaphoreType.DMA((3,)),
            pltpu.SemaphoreType.DMA((3,)),
        ],
        compiler_params=pltpu.CompilerParams(
            collective_id=0, has_side_effects=True, vmem_limit_bytes=32 * 1024 * 1024
        ),
    )(facet_positions, reflectivity, block_building, visible, platform)


def solution(mesh):
    return jax.shard_map(
        body,
        mesh=mesh,
        in_specs=(P(None, "facet"), P(None, "facet"), P("facet"), P(None, "pulse"), P(None, "pulse")),
        out_specs=P(None, "pulse", "facet"),
        check_vma=False,
    )
```

```python
import functools
import math

import jax
import jax.numpy as jnp
from jax import lax
from jax.experimental import pallas as pl
from jax.experimental.pallas import tpu as pltpu
from jax.sharding import PartitionSpec as P

PULSES = 2048
F32 = jnp.float32
BF16 = jnp.bfloat16
TILES = 6
TURN = 1.0 / (2.0 * math.pi)

SIN_POLY = (3.1415926401307086, -5.167710083507905, 2.5500775232148403, -0.5982912856219295, 0.07765766030867731)
COS_POLY = (0.9999999532476086, -4.934792830619651, 4.058411352862725, -1.3318765680816778, 0.21968961109948743)


def horner(q, coefs):
    out = jnp.full_like(q, coefs[-1])
    for c in coefs[-2::-1]:
        out = out * q + c
    return out


def cos_sin_turns(u):
    r = u - jnp.round(u)
    q = r * r
    s = horner(q, SIN_POLY) * r
    c = horner(q, COS_POLY)
    t = s + s
    return 1.0 - t * s, t * c


def iota(shape, dim):
    return lax.broadcasted_iota(jnp.int32, shape, dim)


def kernel(
    fp_hbm, rf_hbm, bb_hbm, vis_hbm, plat_hbm, out_ref,
    fp, rf, bb, vis, plat, pcols, wts, ta, tb, own, send0, recv0, send2, recv2, send3, recv3,
    tdft, twid, vdft, chirp, in_sem, send_sem, recv_sem,
):
    j = lax.axis_index("facet")
    i = lax.axis_index("pulse")
    chip, core = j // 2, j % 2
    xh, z = i // 16, i % 16
    sibling = {"facet": chip * 2 + 1 - core, "pulse": i}

    ins = [
        pltpu.make_async_copy(src, dst, in_sem.at[n])
        for n, (src, dst) in enumerate(
            ((plat_hbm, plat), (fp_hbm, fp), (bb_hbm, bb), (vis_hbm, vis), (rf_hbm, rf))
        )
    ]
    for c in ins:
        c.start()

    def remote(src, dst, k, device):
        return pltpu.make_async_remote_copy(
            src_ref=src, dst_ref=dst, send_sem=send_sem.at[k], recv_sem=recv_sem.at[k],
            device_id=device, device_id_type=pl.DeviceIdType.MESH,
        )

    barrier = pltpu.get_barrier_semaphore()

    def greet(device):
        pl.semaphore_signal(
            barrier, inc=1, device_id=device, device_id_type=pl.DeviceIdType.MESH
        )

    for t in (8, 7, 9, 6, 10, 5, 11, 4, 12, 3, 13, 2, 14, 1, 15):
        greet({"facet": j, "pulse": 16 * xh + (z + t) % 16})
    for r in (1, 0):
        for t in range(7, -1, -1):
            source = {"facet": (chip + t) % 8 * 2 + xh, "pulse": 16 * ((xh + r) % 2) + z}
            if t or r:
                greet(source)
            else:
                pl.when(core != xh)(functools.partial(greet, source))
    greet(sibling)

    for c in ins:
        c.wait()
    eye = iota((64, 64), 0) == iota((64, 64), 1)
    for d in range(3):
        column = jnp.sum(jnp.where(eye, plat[d : d + 1, :], 0.0), axis=1, keepdims=True)
        pcols[d] = jnp.broadcast_to(column, (64, 128))
    for blk in range(TILES):
        b = bb[blk]
        cols = pl.ds(blk * 128, 128)
        for h in range(2):
            seen = vis[h, b].astype(F32)
            wts[h, :, cols] = rf[:, cols] * seen

    lane = iota((128, 128), 1)
    same_pulse = (iota((128, 128), 0) % 8) == (lane % 8)
    fold = (iota((16, 128), 0) == iota((16, 128), 1) // 8).astype(BF16)
    scale_u = 0.125 * TURN
    for g in range(8):
        rows = slice(g * 8, g * 8 + 8)
        px, py, pz = pcols[0, rows, :], pcols[1, rows, :], pcols[2, rows, :]
        half = g // 4
        buf = g % 2
        for n in range(TILES):
            cols = pl.ds(n * 128, 128)
            dx = fp[0:1, cols] - px
            dy = fp[1:2, cols] - py
            dz = fp[2:3, cols] - pz
            d2 = dx * dx + dy * dy + dz * dz
            u = jnp.sqrt(d2) * scale_u
            w0 = wts[half, 0:1, cols]
            w1 = wts[half, 1:2, cols]
            c0, s0 = cos_sin_turns(u)
            cz, sz = cos_sin_turns(64.0 * u)
            two = 4.0 * (c0 * c0) - 2.0
            cb, sb = [c0], [s0]
            cp, sp = c0, -s0
            for _ in range(15):
                cn, sn = two * cb[-1] - cp, two * sb[-1] - sp
                cp, sp = cb[-1], sb[-1]
                cb.append(cn)
                sb.append(sn)
            arp, aip = w0 * cb[8] - w1 * sb[8], w1 * cb[8] + w0 * sb[8]
            ar = [arp * cz + aip * sz]
            ai = [aip * cz - arp * sz]
            two_z = cz + cz
            for _ in range(15):
                rn, im = two_z * ar[-1] - arp, two_z * ai[-1] - aip
                arp, aip = ar[-1], ai[-1]
                ar.append(rn)
                ai.append(im)
            for m in range(0, 16, 2):
                r16 = slice(m * 8, m * 8 + 16)
                q16 = slice(128 + m * 8, 128 + m * 8 + 16)
                tb[buf, r16, cols] = jnp.concatenate([cb[m], cb[m + 1]], axis=0).astype(BF16)
                tb[buf, q16, cols] = jnp.concatenate([sb[m], sb[m + 1]], axis=0).astype(BF16)
                ta[buf, r16, cols] = jnp.concatenate([ar[m], ar[m + 1]], axis=0).astype(BF16)
                ta[buf, q16, cols] = jnp.concatenate([ai[m], ai[m + 1]], axis=0).astype(BF16)
        prod = lax.dot_general(
            ta[buf], tb[buf], (((1,), (1,)), ((), ())), preferred_element_type=F32
        )
        rc, rs = prod[:128, :128], prod[:128, 128:]
        ic, is_ = prod[128:, :128], prod[128:, 128:]
        parts = []
        for comp in (rc - is_, ic + rs, rc + is_, ic - rs):
            parts.append(jnp.where(same_pulse, comp, 0.0).astype(BF16))
        echo = lax.dot_general(
            fold, jnp.concatenate(parts, axis=1), (((1,), (0,)), ((), ())),
            preferred_element_type=F32,
        )
        mine = jnp.where(core == 0, echo[:8], echo[8:])
        other = jnp.where(core == 0, echo[8:], echo[:8])
        for comp in range(4):
            own[g * 32 + comp * 8 : g * 32 + comp * 8 + 8, :] = mine[:, comp * 128 : comp * 128 + 128]
        for pair in range(2):
            a = other[:, pair * 256 : pair * 256 + 128]
            b = other[:, pair * 256 + 128 : pair * 256 + 256]
            send0[g, pair * 16 : pair * 16 + 16, :] = jnp.concatenate([a, b], axis=0).astype(BF16)

    lanes = iota((16, 256), 1)
    pulse8 = (8 * (16 * xh + (z + 1 + lanes // 16) % 16) + lanes % 8).astype(F32)
    real_col = lanes // 8 % 2 == 0

    def dft_rows(m, carry):
        k = (m * 16 + iota((16, 256), 0)).astype(F32)
        c, s = cos_sin_turns(k * pulse8 * (1.0 / 256.0))
        rows = pl.ds(pl.multiple_of(m * 16, 16), 16)
        rows_i = pl.ds(pl.multiple_of(256 + m * 16, 16), 16)
        tdft[rows, :] = jnp.where(real_col, c, s).astype(BF16)
        tdft[rows_i, :] = jnp.where(real_col, -s, c).astype(BF16)
        kt = (m * 16 + iota((16, 128), 0)).astype(F32)
        pt = (iota((16, 128), 1) % 8).astype(F32)
        c, s = cos_sin_turns(kt * pt * (1.0 / PULSES))
        twid[0, rows, :] = c
        twid[1, rows, :] = s
        return carry

    lax.fori_loop(0, 16, dft_rows, 0)

    row = iota((16, 256), 0)
    col = iota((16, 256), 1)
    bin_here = jnp.where(z % 2 == 1, row, 15 - row)
    same_bin = col // 8 % 16 == bin_here
    for h in range(8):
        c, s = cos_sin_turns((h * (col % 8)).astype(F32) * 0.125)
        first = col < 128
        vdft[h * 16 : h * 16 + 16, :] = jnp.where(same_bin, jnp.where(first, c, s), 0.0).astype(BF16)
        vdft[128 + h * 16 : 144 + h * 16, :] = jnp.where(
            same_bin, jnp.where(first, -s, c), 0.0
        ).astype(BF16)

    kk = (j * 128 - PULSES // 2 + iota((16, 128), 1)).astype(F32)
    ff = (i * 16 + iota((16, 128), 0)).astype(F32)
    ch_c, ch_s = cos_sin_turns(kk * kk * (1.0 / PULSES) / (2.0 + 0.25 * ff))
    chirp[0] = ch_c * (1.0 / math.sqrt(PULSES))
    chirp[1] = ch_s * (1.0 / math.sqrt(PULSES))

    pl.semaphore_wait(barrier, jnp.where(core == xh, 31, 32))

    pair_copy = remote(send0, recv0, 0, sibling)
    pair_copy.start()
    pair_copy.wait_recv()
    for g in range(8):
        rows = slice(g * 32, g * 32 + 32)
        own[rows, :] = own[rows, :] + recv0[g].astype(F32)

    for a in range(8):
        for sign in range(2):
            piece = [own[pl.ds(sign * 16 + c * 8 + a, 8, stride=32), :] for c in range(2)]
            send2[2 * a + sign] = jnp.concatenate(piece, axis=0).astype(BF16)
    for t in (8, 7, 9, 6, 10, 5, 11, 4, 12, 3, 13, 2, 14, 1, 15):
        zd = (z + t) % 16
        remote(send2.at[zd], recv2.at[15 - t], 1, {"facet": j, "pulse": 16 * xh + zd}).start()
    recv2[15] = send2[z]
    first15 = recv2.at[pl.ds(0, 15)]
    got2 = remote(first15, first15, 1, sibling)
    got2.wait_recv()

    held = recv2[...].reshape(256, 128)
    low = jnp.dot(tdft[...], held, preferred_element_type=F32)
    lr, li = low[:256], low[256:]
    tr, ts = twid[0], twid[1]
    turned = jnp.concatenate([lr * tr + li * ts, li * tr - lr * ts], axis=1).astype(BF16)
    spec = lax.dot_general(
        vdft[...], turned, (((1,), (1,)), ((), ())), preferred_element_type=F32
    )
    for h in range(8):
        for odd in range(2):
            cols = slice(odd * 128, odd * 128 + 128)
            send3[2 * h + odd] = jnp.concatenate(
                [spec[h * 16 : h * 16 + 16, cols], spec[128 + h * 16 : 144 + h * 16, cols]], axis=0
            ).astype(BF16)

    place = recv3.at[8 * xh + chip]
    to_self = core == xh
    for t in range(15, 0, -1):
        jd = (j + t) % 16
        remote(send3.at[jd], place, 2, {"facet": jd, "pulse": 16 * core + z}).start()

    @pl.when(to_self)
    def _():
        pltpu.make_async_copy(send3.at[j], place, recv_sem.at[2]).start()

    @pl.when(jnp.logical_not(to_self))
    def _():
        remote(send3.at[j], place, 2, {"facet": j, "pulse": 16 * core + z}).start()

    got3 = remote(send3, recv3, 2, sibling)
    got3.wait_recv()
    total = recv3[0].astype(F32)
    for n in range(1, 16):
        total = total + recv3[n].astype(F32)
    re, im = total[:16], total[16:]
    out_ref[0] = chirp[0] * re - chirp[1] * im
    out_ref[1] = chirp[0] * im + chirp[1] * re

    pair_copy.wait_send()
    got2.wait_send()

    @pl.when(to_self)
    def _():
        most = send3.at[pl.ds(0, 15)]
        remote(most, most, 2, sibling).wait_send()

    @pl.when(jnp.logical_not(to_self))
    def _():
        got3.wait_send()


def body(facet_positions, reflectivity, block_building, visible, platform):
    anywhere = pl.BlockSpec(memory_space=pltpu.HBM)
    return pl.pallas_call(
        kernel,
        out_shape=jax.ShapeDtypeStruct((2, 16, 128), F32),
        in_specs=[anywhere] * 5,
        out_specs=pl.BlockSpec(memory_space=pltpu.VMEM),
        scratch_shapes=[
            pltpu.VMEM((3, 768), F32),
            pltpu.VMEM((2, 768), F32),
            pltpu.SMEM((6,), jnp.int32),
            pltpu.SMEM((2, 24), jnp.int32),
            pltpu.VMEM((3, 64), F32),
            pltpu.VMEM((3, 64, 128), F32),
            pltpu.VMEM((2, 2, 768), F32),
            pltpu.VMEM((2, 256, 768), BF16),
            pltpu.VMEM((2, 256, 768), BF16),
            pltpu.VMEM((256, 128), F32),
            pltpu.VMEM((8, 32, 128), BF16),
            pltpu.VMEM((8, 32, 128), BF16),
            pltpu.VMEM((16, 16, 128), BF16),
            pltpu.VMEM((16, 16, 128), BF16),
            pltpu.VMEM((16, 32, 128), BF16),
            pltpu.VMEM((16, 32, 128), BF16),
            pltpu.VMEM((512, 256), BF16),
            pltpu.VMEM((2, 256, 128), F32),
            pltpu.VMEM((256, 256), BF16),
            pltpu.VMEM((2, 16, 128), F32),
            pltpu.SemaphoreType.DMA((5,)),
            pltpu.SemaphoreType.DMA((3,)),
            pltpu.SemaphoreType.DMA((3,)),
        ],
        compiler_params=pltpu.CompilerParams(
            collective_id=0, has_side_effects=True, vmem_limit_bytes=62 * 1024 * 1024
        ),
    )(facet_positions, reflectivity, block_building, visible.T, platform)


def solution(mesh):
    return jax.shard_map(
        body,
        mesh=mesh,
        in_specs=(P(None, "facet"), P(None, "facet"), P("facet"), P(None, "pulse"), P(None, "pulse")),
        out_specs=P(None, "pulse", "facet"),
        check_vma=False,
    )
```

```python
import functools
import math

import jax
import jax.numpy as jnp
from jax import lax
from jax.experimental import pallas as pl
from jax.experimental.pallas import tpu as pltpu
from jax.sharding import PartitionSpec as P

PULSES = 2048
F32 = jnp.float32
BF16 = jnp.bfloat16
TILES = 6
TURN = 1.0 / (2.0 * math.pi)

SIN_POLY = (3.1415926401307086, -5.167710083507905, 2.5500775232148403, -0.5982912856219295, 0.07765766030867731)
COS_POLY = (0.9999999532476086, -4.934792830619651, 4.058411352862725, -1.3318765680816778, 0.21968961109948743)


def horner(q, coefs):
    out = jnp.full_like(q, coefs[-1])
    for c in coefs[-2::-1]:
        out = out * q + c
    return out


def cos_sin_turns(u):
    r = u - jnp.round(u)
    q = r * r
    s = horner(q, SIN_POLY) * r
    c = horner(q, COS_POLY)
    t = s + s
    return 1.0 - t * s, t * c


def iota(shape, dim):
    return lax.broadcasted_iota(jnp.int32, shape, dim)


def kernel(
    fp_hbm, rf_hbm, bb_hbm, vis_hbm, plat_hbm, out_ref,
    fp, rf, bb, vis, plat, pcols, wts, ta, tb, own, send0, recv0, send2, recv2, send3, recv3,
    tdft, twid, vdft, chirp, prods, masked, in_sem, send_sem, recv_sem,
):
    j = lax.axis_index("facet")
    i = lax.axis_index("pulse")
    chip, core = j // 2, j % 2
    xh, z = i // 16, i % 16
    sibling = {"facet": chip * 2 + 1 - core, "pulse": i}

    def remote(src, dst, k, device):
        return pltpu.make_async_remote_copy(
            src_ref=src, dst_ref=dst, send_sem=send_sem.at[k], recv_sem=recv_sem.at[k],
            device_id=device, device_id_type=pl.DeviceIdType.MESH,
        )

    barrier = pltpu.get_barrier_semaphore()

    def greet(device):
        pl.semaphore_signal(
            barrier, inc=1, device_id=device, device_id_type=pl.DeviceIdType.MESH
        )

    for t in (8, 7, 9, 6, 10, 5, 11, 4, 12, 3, 13, 2, 14, 1, 15):
        greet({"facet": j, "pulse": 16 * xh + (z + t) % 16})
    for r in (1, 0):
        for t in range(7, -1, -1):
            source = {"facet": (chip + t) % 8 * 2 + xh, "pulse": 16 * ((xh + r) % 2) + z}
            if t or r:
                greet(source)
            else:
                pl.when(core != xh)(functools.partial(greet, source))
    greet(sibling)

    ins = [
        pltpu.make_async_copy(src, dst, in_sem.at[n])
        for n, (src, dst) in enumerate(
            ((plat_hbm, plat), (fp_hbm, fp), (bb_hbm, bb), (vis_hbm, vis), (rf_hbm, rf))
        )
    ]
    for c in ins:
        c.start()

    lanes = iota((16, 256), 1)
    pulse8 = (8 * (16 * xh + (z + 1 + lanes // 16) % 16) + lanes % 8).astype(F32)
    real_col = lanes // 8 % 2 == 0

    def dft_rows(m, carry):
        k = (m * 16 + iota((16, 256), 0)).astype(F32)
        c, s = cos_sin_turns(k * pulse8 * (1.0 / 256.0))
        rows = pl.ds(pl.multiple_of(m * 16, 16), 16)
        rows_i = pl.ds(pl.multiple_of(256 + m * 16, 16), 16)
        tdft[rows, :] = jnp.where(real_col, c, s).astype(BF16)
        tdft[rows_i, :] = jnp.where(real_col, -s, c).astype(BF16)
        kt = (m * 16 + iota((16, 128), 0)).astype(F32)
        pt = (iota((16, 128), 1) % 8).astype(F32)
        c, s = cos_sin_turns(kt * pt * (1.0 / PULSES))
        twid[0, rows, :] = c
        twid[1, rows, :] = s
        return carry

    lax.fori_loop(0, 16, dft_rows, 0)

    row = iota((16, 256), 0)
    col = iota((16, 256), 1)
    bin_here = jnp.where(z % 2 == 1, row, 15 - row)
    same_bin = col // 8 % 16 == bin_here
    for h in range(8):
        c, s = cos_sin_turns((h * (col % 8)).astype(F32) * 0.125)
        first = col < 128
        vdft[h * 16 : h * 16 + 16, :] = jnp.where(same_bin, jnp.where(first, c, s), 0.0).astype(BF16)
        vdft[128 + h * 16 : 144 + h * 16, :] = jnp.where(
            same_bin, jnp.where(first, -s, c), 0.0
        ).astype(BF16)

    kk = (j * 128 - PULSES // 2 + iota((16, 128), 1)).astype(F32)
    ff = (i * 16 + iota((16, 128), 0)).astype(F32)
    ch_c, ch_s = cos_sin_turns(kk * kk * (1.0 / PULSES) / (2.0 + 0.25 * ff))
    chirp[0] = ch_c * (1.0 / math.sqrt(PULSES))
    chirp[1] = ch_s * (1.0 / math.sqrt(PULSES))

    for c in ins:
        c.wait()
    eye = iota((64, 64), 0) == iota((64, 64), 1)
    for d in range(3):
        column = jnp.sum(jnp.where(eye, plat[d : d + 1, :], 0.0), axis=1, keepdims=True)
        pcols[d] = jnp.broadcast_to(column, (64, 128))
    for blk in range(TILES):
        b = bb[blk]
        cols = pl.ds(blk * 128, 128)
        for h in range(2):
            seen = vis[h, b].astype(F32)
            wts[h, :, cols] = rf[:, cols] * seen

    lane = iota((128, 128), 1)
    same_pulse = (iota((128, 128), 0) % 8) == (lane % 8)
    fold = (iota((16, 128), 0) == iota((16, 128), 1) // 8).astype(BF16)
    scale_u = 0.125 * TURN
    def make_tables(g):
        rows = slice(g * 8, g * 8 + 8)
        px, py, pz = pcols[0, rows, :], pcols[1, rows, :], pcols[2, rows, :]
        half = g // 4
        buf = g % 2
        for n in range(TILES):
            cols = pl.ds(n * 128, 128)
            dx = fp[0:1, cols] - px
            dy = fp[1:2, cols] - py
            dz = fp[2:3, cols] - pz
            d2 = dx * dx + dy * dy + dz * dz
            u = jnp.sqrt(d2) * scale_u
            w0 = wts[half, 0:1, cols]
            w1 = wts[half, 1:2, cols]
            c0, s0 = cos_sin_turns(u)
            cz, sz = cos_sin_turns(64.0 * u)
            two = 4.0 * (c0 * c0) - 2.0
            cb, sb = [c0], [s0]
            cp, sp = c0, -s0
            for _ in range(15):
                cn, sn = two * cb[-1] - cp, two * sb[-1] - sp
                cp, sp = cb[-1], sb[-1]
                cb.append(cn)
                sb.append(sn)
            arp, aip = w0 * cb[8] - w1 * sb[8], w1 * cb[8] + w0 * sb[8]
            ar = [arp * cz + aip * sz]
            ai = [aip * cz - arp * sz]
            two_z = cz + cz
            for _ in range(15):
                rn, im = two_z * ar[-1] - arp, two_z * ai[-1] - aip
                arp, aip = ar[-1], ai[-1]
                ar.append(rn)
                ai.append(im)
            for m in range(0, 16, 2):
                r16 = slice(m * 8, m * 8 + 16)
                q16 = slice(128 + m * 8, 128 + m * 8 + 16)
                tb[buf, r16, cols] = jnp.concatenate([cb[m], cb[m + 1]], axis=0).astype(BF16)
                tb[buf, q16, cols] = jnp.concatenate([sb[m], sb[m + 1]], axis=0).astype(BF16)
                ta[buf, r16, cols] = jnp.concatenate([ar[m], ar[m + 1]], axis=0).astype(BF16)
                ta[buf, q16, cols] = jnp.concatenate([ai[m], ai[m + 1]], axis=0).astype(BF16)

    def products(g):
        buf = g % 2
        return lax.dot_general(
            ta[buf], tb[buf], (((1,), (1,)), ((), ())), preferred_element_type=F32
        )

    def kept(prod):
        rc, rs = prod[:128, :128], prod[:128, 128:]
        ic, is_ = prod[128:, :128], prod[128:, 128:]
        parts = []
        for comp in (rc - is_, ic + rs, rc + is_, ic - rs):
            parts.append(jnp.where(same_pulse, comp, 0.0).astype(BF16))
        return jnp.concatenate(parts, axis=1)

    def fold_up(g, parts):
        echo = lax.dot_general(
            fold, parts, (((1,), (0,)), ((), ())),
            preferred_element_type=F32,
        )
        mine = jnp.where(core == 0, echo[:8], echo[8:])
        other = jnp.where(core == 0, echo[8:], echo[:8])
        for comp in range(4):
            own[g * 32 + comp * 8 : g * 32 + comp * 8 + 8, :] = mine[:, comp * 128 : comp * 128 + 128]
        for pair in range(2):
            a = other[:, pair * 256 : pair * 256 + 128]
            b = other[:, pair * 256 + 128 : pair * 256 + 256]
            send0[g, pair * 16 : pair * 16 + 16, :] = jnp.concatenate([a, b], axis=0).astype(BF16)


    make_tables(0)
    for g in range(9):
        if g < 8:
            prods[g % 2] = products(g)
        if g < 7:
            make_tables(g + 1)
        if g > 0:
            fold_up(g - 1, masked[(g - 1) % 2])
        if g < 8:
            masked[g % 2] = kept(prods[g % 2])

    pl.semaphore_wait(barrier, jnp.where(core == xh, 31, 32))

    pair_copy = remote(send0, recv0, 0, sibling)
    pair_copy.start()
    pair_copy.wait_recv()
    for g in range(8):
        rows = slice(g * 32, g * 32 + 32)
        own[rows, :] = own[rows, :] + recv0[g].astype(F32)

    for a in range(8):
        for sign in range(2):
            piece = [own[pl.ds(sign * 16 + c * 8 + a, 8, stride=32), :] for c in range(2)]
            send2[2 * a + sign] = jnp.concatenate(piece, axis=0).astype(BF16)
    for t in (8, 7, 9, 6, 10, 5, 11, 4, 12, 3, 13, 2, 14, 1, 15):
        zd = (z + t) % 16
        remote(send2.at[zd], recv2.at[15 - t], 1, {"facet": j, "pulse": 16 * xh + zd}).start()
    recv2[15] = send2[z]
    first15 = recv2.at[pl.ds(0, 15)]
    got2 = remote(first15, first15, 1, sibling)
    got2.wait_recv()

    held = recv2[...].reshape(256, 128)
    low = jnp.dot(tdft[...], held, preferred_element_type=F32)
    lr, li = low[:256], low[256:]
    tr, ts = twid[0], twid[1]
    turned = jnp.concatenate([lr * tr + li * ts, li * tr - lr * ts], axis=1).astype(BF16)
    spec = lax.dot_general(
        vdft[...], turned, (((1,), (1,)), ((), ())), preferred_element_type=F32
    )
    for h in range(8):
        for odd in range(2):
            cols = slice(odd * 128, odd * 128 + 128)
            send3[2 * h + odd] = jnp.concatenate(
                [spec[h * 16 : h * 16 + 16, cols], spec[128 + h * 16 : 144 + h * 16, cols]], axis=0
            ).astype(BF16)

    place = recv3.at[8 * xh + chip]
    to_self = core == xh
    for t in range(15, 0, -1):
        jd = (j + t) % 16
        remote(send3.at[jd], place, 2, {"facet": jd, "pulse": 16 * core + z}).start()

    @pl.when(to_self)
    def _():
        pltpu.make_async_copy(send3.at[j], place, recv_sem.at[2]).start()

    @pl.when(jnp.logical_not(to_self))
    def _():
        remote(send3.at[j], place, 2, {"facet": j, "pulse": 16 * core + z}).start()

    got3 = remote(send3, recv3, 2, sibling)
    got3.wait_recv()
    total = recv3[0].astype(F32)
    for n in range(1, 16):
        total = total + recv3[n].astype(F32)
    re, im = total[:16], total[16:]
    out_ref[0] = chirp[0] * re - chirp[1] * im
    out_ref[1] = chirp[0] * im + chirp[1] * re

    pair_copy.wait_send()
    got2.wait_send()

    @pl.when(to_self)
    def _():
        most = send3.at[pl.ds(0, 15)]
        remote(most, most, 2, sibling).wait_send()

    @pl.when(jnp.logical_not(to_self))
    def _():
        got3.wait_send()


def body(facet_positions, reflectivity, block_building, visible, platform):
    args = (facet_positions, reflectivity, block_building, visible.T, platform)
    anywhere = pl.BlockSpec(memory_space=pltpu.HBM)
    return pl.pallas_call(
        kernel,
        out_shape=jax.ShapeDtypeStruct((2, 16, 128), F32),
        in_specs=[anywhere] * 5,
        out_specs=pl.BlockSpec(memory_space=pltpu.VMEM),
        scratch_shapes=[
            pltpu.VMEM((3, 768), F32),
            pltpu.VMEM((2, 768), F32),
            pltpu.SMEM((6,), jnp.int32),
            pltpu.SMEM((2, 24), jnp.int32),
            pltpu.VMEM((3, 64), F32),
            pltpu.VMEM((3, 64, 128), F32),
            pltpu.VMEM((2, 2, 768), F32),
            pltpu.VMEM((2, 256, 768), BF16),
            pltpu.VMEM((2, 256, 768), BF16),
            pltpu.VMEM((256, 128), F32),
            pltpu.VMEM((8, 32, 128), BF16),
            pltpu.VMEM((8, 32, 128), BF16),
            pltpu.VMEM((16, 16, 128), BF16),
            pltpu.VMEM((16, 16, 128), BF16),
            pltpu.VMEM((16, 32, 128), BF16),
            pltpu.VMEM((16, 32, 128), BF16),
            pltpu.VMEM((512, 256), BF16),
            pltpu.VMEM((2, 256, 128), F32),
            pltpu.VMEM((256, 256), BF16),
            pltpu.VMEM((2, 16, 128), F32),
            pltpu.VMEM((2, 256, 256), F32),
            pltpu.VMEM((2, 128, 512), BF16),
            pltpu.SemaphoreType.DMA((5,)),
            pltpu.SemaphoreType.DMA((3,)),
            pltpu.SemaphoreType.DMA((3,)),
        ],
        compiler_params=pltpu.CompilerParams(
            collective_id=0, has_side_effects=True, vmem_limit_bytes=48 * 1024 * 1024
        ),
    )(*[pltpu.with_memory_space_constraint(x, pltpu.HBM) for x in args])


def solution(mesh):
    return jax.shard_map(
        body,
        mesh=mesh,
        in_specs=(P(None, "facet"), P(None, "facet"), P("facet"), P(None, "pulse"), P(None, "pulse")),
        out_specs=P(None, "pulse", "facet"),
        check_vma=False,
    )
```
